32 devices in a mesh: replica: 8 (over z, y), shard: 4 (over x, core).
Axes of the slice: x: 2, y: 2, z: 4, core: 2. Of those that a mesh axis runs over, the one named last changes fastest.
Arguments:
- tokens: bfloat16 [32768, 1024], P(('replica', 'shard')), may hold values from -6 to 6
- lengths: int32 [32, 3], P(('replica', 'shard')), may hold values from 1 to 512, 1024 in all within a row
- attention_gain: bfloat16 [1024], P('shard'), may hold values from 0.5 to 1.5
- query_weight: bfloat16 [1024, 2048], P('shard'), may hold values from -0.1875 to 0.1875
- key_weight: bfloat16 [1024, 1024], P('shard'), may hold values from -0.1875 to 0.1875
- value_weight: bfloat16 [1024, 1024], P('shard'), may hold values from -0.1875 to 0.1875
- query_gain: bfloat16 [128], P('shard'), may hold values from 0.5 to 1.5
- key_gain: bfloat16 [128], P('shard'), may hold values from 0.5 to 1.5
- output_weight: bfloat16 [2048, 1024], P('shard'), may hold values from -1 to 1
- feedforward_gain: bfloat16 [1024], P('shard'), may hold values from 0.5 to 1.5
- gate_weight: bfloat16 [1024, 3072], P('shard'), may hold values from -0.1875 to 0.1875
- up_weight: bfloat16 [1024, 3072], P('shard'), may hold values from -0.1875 to 0.1875
- down_weight: bfloat16 [3072, 1024], P('shard'), may hold values from -0.109375 to 0.109375
- cotangent: bfloat16 [32768, 1024], P(('replica', 'shard')), may hold values from -6 to 6
Outputs:
- mixed: bfloat16 [32768, 1024], P(('replica', 'shard'))
- grad_tokens: float32 [32768, 1024], P(('replica', 'shard'))
- grad_attention_gain: float32 [1024], P('shard')
- grad_query_weight: float32 [1024, 2048], P('shard')
- grad_key_weight: float32 [1024, 1024], P('shard')
- grad_value_weight: float32 [1024, 1024], P('shard')
- grad_query_gain: float32 [128], P('shard')
- grad_key_gain: float32 [128], P('shard')
- grad_output_weight: float32 [2048, 1024], P('shard')
- grad_feedforward_gain: float32 [1024], P('shard')
- grad_gate_weight: float32 [1024, 3072], P('shard')
- grad_up_weight: float32 [1024, 3072], P('shard')
- grad_down_weight: float32 [3072, 1024], P('shard')
The draws below stay inside these ranges and needn't reach their ends.
Inputs may be any that keep to these rules, and one draw needn't show every extreme that they name: Each row holds 3 document lengths that sum to 1024; the longest of each row is exactly 512.
All inputs are finite; a program needn't handle non-finite values.
Results may differ from the reference program's by a relative error of at most 0.02.
Values may be sent and summed in bfloat16 or wider, within the bound.
A program may use at most 384 MiB of HBM per device.

```python
import math
import jax
import jax.numpy as jnp
import numpy as np
from jax import lax

D = 1024
H = 16
KV = 8
HD = 128
FF = 3072
SEQ_LEN = 1024
DOCS = 3
MOST = 512
SEQS = 32
TOKENS = 32768


def block_scale(stream_key, extent, split, least, high):
    loudness, own = 1.0, jax.random.fold_in(stream_key, 6)
    for dim, shards_of in split:
        steps = jnp.exp(jax.random.uniform(jax.random.fold_in(own, dim), (shards_of,), jnp.float32, least / len(split), high / len(split)))
        loudness = loudness * jnp.repeat(steps, extent[dim] // shards_of).reshape([-1 if axis == dim else 1 for axis in range(len(extent))])
    return loudness


def length_profile(count, total, limit, lean):
    portions = [(1 << 20) // math.isqrt(rank ** lean) + 1 for rank in range(2, count + 1)]
    surplus, holding = total - limit - (count - 1), [1] * (count - 1)
    while surplus > 0:
        movable = [i for i in range(count - 1) if holding[i] < limit]
        pool, left = sum([portions[i] for i in movable]), surplus
        for i in movable:
            extra = min(limit - holding[i], max(1, left * portions[i] // pool), surplus)
            holding[i] = holding[i] + extra
            surplus = surplus - extra
    return np.array([limit] + holding)


def uneven_parts(own_key, amount, total, bound, skew):
    if amount == 2:
        one = jax.random.randint(own_key, (), max(1, total - bound), min(bound, total - 1) + 1)
        return jnp.stack([one, total - one])
    sizes = jnp.asarray(length_profile(amount, total, bound, skew), jnp.int32)
    twos = (amount - 1) // 2
    giver, receiver = sizes[1:1 + 2 * twos:2], sizes[2:2 + 2 * twos:2]
    room = jnp.minimum(giver - 1, bound - receiver)
    moved = jax.random.randint(jax.random.fold_in(own_key, 1), (twos,), 0, 1 << 20) % (room + 1)
    sizes = sizes.at[1:1 + 2 * twos:2].set(giver - moved).at[2:2 + 2 * twos:2].set(receiver + moved)
    return sizes[jax.random.permutation(jax.random.fold_in(own_key, 2), amount)]


def noise(stream_key, dims, scale, bound, cuts=(), held_as=jnp.bfloat16):
    loudness = block_scale(stream_key, dims, cuts, -0.22, 0.18) if cuts else 1.0
    values = jax.random.normal(stream_key, dims, jnp.float32) * scale * loudness
    return jnp.minimum(jnp.maximum(values, -bound), bound).astype(held_as)


def setup_inputs(seed: int = 0) -> dict:
    splits = jax.random.split(jax.random.key(seed), 15)
    tokens = noise(splits[0], (TOKENS, D), 1.0, 6.0, ((0, 32),))
    lengths = jax.vmap(lambda own: uneven_parts(own, DOCS, SEQ_LEN, MOST, 1))(jax.random.split(splits[1], SEQS)).reshape((SEQS, DOCS)).astype(jnp.int32)
    attention_gain = jnp.clip(1.0 + 0.1 * jax.random.normal(splits[2], (D,), jnp.float32), 0.5, 1.5).astype(jnp.bfloat16)
    query_weight = noise(splits[3], (D, H * HD), D ** -0.5, 0.1875, ((0, 4),))
    key_weight = noise(splits[4], (D, KV * HD), D ** -0.5, 0.1875, ((0, 4),))
    value_weight = noise(splits[5], (D, KV * HD), D ** -0.5, 0.1875, ((0, 4),))
    query_gain = jnp.clip(1.0 + 0.1 * jax.random.normal(splits[6], (HD,), jnp.float32), 0.5, 1.5).astype(jnp.bfloat16)
    key_gain = jnp.clip(1.0 + 0.1 * jax.random.normal(splits[7], (HD,), jnp.float32), 0.5, 1.5).astype(jnp.bfloat16)
    output_weight = noise(splits[8], (H * HD, D), (max(H * HD // 64, 16)) ** -0.5, 1.0, ((0, 4),))
    feedforward_gain = jnp.clip(1.0 + 0.1 * jax.random.normal(splits[9], (D,), jnp.float32), 0.5, 1.5).astype(jnp.bfloat16)
    gate_weight = noise(splits[10], (D, FF), D ** -0.5, 0.1875, ((0, 4),))
    up_weight = noise(splits[11], (D, FF), D ** -0.5, 0.1875, ((0, 4),))
    down_weight = noise(splits[12], (FF, D), FF ** -0.5, 0.109375, ((0, 4),))
    cotangent = noise(splits[13], (TOKENS, D), 1.0, 6.0, ((0, 32),))
    return {"tokens": tokens, "lengths": lengths, "attention_gain": attention_gain, "query_weight": query_weight, "key_weight": key_weight, "value_weight": value_weight, "query_gain": query_gain, "key_gain": key_gain, "output_weight": output_weight, "feedforward_gain": feedforward_gain, "gate_weight": gate_weight, "up_weight": up_weight, "down_weight": down_weight, "cotangent": cotangent}


norm_epsilon = 1e-06
rotary_base = 1000000.0
masked_score = -1e+30

@jax.custom_vjp
def low(v):
    return lax.optimization_barrier(v.astype(jnp.bfloat16)).astype(jnp.float32)

@jax.custom_vjp
def low_back(v):
    return v

def low_keep(v):
    return (low(v), None)

def low_pass(kept, grad):
    return (grad,)

def back_keep(v):
    return (v, None)

def back_low(kept, grad):
    return (low(grad),)
low.defvjp(low_keep, low_pass)
low_back.defvjp(back_keep, back_low)

def doc_layout(lengths, seq_length):
    bounds = jnp.cumsum(lengths, axis=-1).astype(jnp.int32)
    places = lax.broadcasted_iota(jnp.int32, (seq_length,), 0)
    passed = (places[None, :, None] >= bounds[:, None, :]).astype(jnp.int32)
    segment = lax.optimization_barrier(jnp.sum(passed, axis=-1)).astype(jnp.int32)
    begins = lax.optimization_barrier(jnp.sum(passed * lengths[:, None, :], axis=-1)).astype(jnp.int32)
    return (segment, (places[None, :] - begins).astype(jnp.int32))

def rotary_tables(position, head_size):
    halves = jnp.arange(head_size // 2, dtype=jnp.float32)
    frequency = rotary_base ** (-(2.0 / head_size) * halves)
    angles = position.astype(jnp.float32)[..., None] * frequency
    cosine = jnp.cos(angles)
    sine = jnp.sin(angles)
    return (jnp.concatenate([cosine, cosine], -1), jnp.concatenate([sine, sine], -1))

def rotate(vector, cosine, sine):
    middle = vector.shape[-1] // 2
    turned = jnp.concatenate([-vector[..., middle:], vector[..., :middle]], -1)
    return vector * cosine + turned * sine

def rms_norm(value, gain):
    factor = lax.rsqrt(lax.optimization_barrier(jnp.mean(value * value, axis=-1, keepdims=True)) + norm_epsilon)
    return value * factor * gain

def product(left, right):
    return jnp.dot(left, right, precision=lax.Precision.HIGHEST, preferred_element_type=jnp.float32)

def one_sequence(pieces):
    queries, keys, values, segment = pieces
    keys_all = jnp.repeat(keys, H // KV, axis=1)
    values_all = jnp.repeat(values, H // KV, axis=1)
    raw = jnp.einsum('qhd,khd->hqk', queries, keys_all, precision=lax.Precision.HIGHEST)
    scores = low_back(raw * HD ** (-0.5))
    places = lax.broadcasted_iota(jnp.int32, (SEQ_LEN, SEQ_LEN), 0)
    others = lax.broadcasted_iota(jnp.int32, (SEQ_LEN, SEQ_LEN), 1)
    allowed = (segment[:, None] == segment[None, :]) & (others <= places)
    masked = jnp.where(allowed[None], scores, masked_score)
    peak = lax.optimization_barrier(jnp.max(masked, axis=-1, keepdims=True))
    weights = jnp.exp(masked - peak)
    probs = weights / lax.optimization_barrier(jnp.sum(weights, axis=-1, keepdims=True))
    return jnp.einsum('hqk,khd->qhd', low(probs), values_all, precision=lax.Precision.HIGHEST)

def reference(tokens, lengths, attention_gain, query_weight, key_weight, value_weight, query_gain, key_gain, output_weight, feedforward_gain, gate_weight, up_weight, down_weight, cotangent):
    segment, position = doc_layout(lengths, SEQ_LEN)
    cosine, sine = rotary_tables(position, HD)
    cosine = cosine[:, :, None, :]
    sine = sine[:, :, None, :]

    def forward(inputs, gain_one, w_query, w_key, w_value, gain_query, gain_key, w_output, gain_two, w_gate, w_up, w_down):
        normed = low(rms_norm(inputs, gain_one))
        query_raw = low_back(product(normed, w_query)).reshape(SEQS, SEQ_LEN, H, HD)
        key_raw = low_back(product(normed, w_key)).reshape(SEQS, SEQ_LEN, KV, HD)
        values = low(low_back(product(normed, w_value))).reshape(SEQS, SEQ_LEN, KV, HD)
        queries = low(rotate(rms_norm(query_raw, gain_query), cosine, sine))
        keys = low(rotate(rms_norm(key_raw, gain_key), cosine, sine))
        attended = lax.map(jax.checkpoint(one_sequence), (queries, keys, values, segment))
        attended = low(low_back(attended.reshape(TOKENS, H * HD)))
        middle = inputs + low_back(product(attended, w_output))
        normed_two = low(rms_norm(middle, gain_two))
        gate_value = low_back(product(normed_two, w_gate))
        up_value = low_back(product(normed_two, w_up))
        hidden = low(gate_value * jax.nn.sigmoid(gate_value) * up_value)
        return middle + low_back(product(hidden, w_down))
    params = tuple((item.astype(jnp.float32) for item in (attention_gain, query_weight, key_weight, value_weight, query_gain, key_gain, output_weight, feedforward_gain, gate_weight, up_weight, down_weight)))
    output, pullback = jax.vjp(forward, tokens.astype(jnp.float32), *params)
    grads = pullback(cotangent.astype(jnp.float32))
    return (output.astype(jnp.bfloat16), grads[0], grads[1], grads[2], grads[3], grads[4], grads[5], grads[6], grads[7], grads[8], grads[9], grads[10], grads[11])
```

```python
import jax
import jax.numpy as jnp
from jax import lax
from jax.experimental import pallas as pl
from jax.experimental.pallas import tpu as pltpu
from jax.sharding import PartitionSpec as P

H = 16
KV = 8
HD = 128
SEQ_LEN = 1024
LONGEST = 512
ROWS = 256
WINDOW = LONGEST + ROWS
PARTS = 1
PAIR = H // KV * HD
VMEM_LIMIT = 56 * 1024 * 1024


norm_epsilon = 1e-06
rotary_base = 1000000.0


def doc_layout(lengths, seq_length):
    bounds = jnp.cumsum(lengths, axis=-1)
    places = lax.broadcasted_iota(jnp.int32, (seq_length,), 0)
    passed = (places[None, :, None] >= bounds[:, None, :]).astype(jnp.int32)
    segment = jnp.sum(passed, axis=-1)
    begins = jnp.sum(passed * lengths[:, None, :], axis=-1)
    return (segment, places[None, :] - begins)


def rotary_tables(position, head_size):
    halves = jnp.arange(head_size // 2, dtype=jnp.float32)
    frequency = rotary_base ** (-(2.0 / head_size) * halves)
    angles = position.astype(jnp.float32)[..., None] * frequency
    cosine = jnp.cos(angles)
    sine = jnp.sin(angles)
    return (jnp.concatenate([cosine, cosine], -1), jnp.concatenate([sine, sine], -1))


def norm_forward(value, gain):
    factor = lax.rsqrt(jnp.mean(value * value, axis=-1, keepdims=True) + norm_epsilon)
    return (value * factor * gain, factor)


def norm_backward(value, factor, gain, gradient):
    scaled = gradient * gain
    inner = jnp.mean(scaled * value, axis=-1, keepdims=True)
    return (factor * (scaled - value * factor * factor * inner), gradient * value * factor)


def dot(left, right):
    return jnp.dot(left, right, preferred_element_type=jnp.float32)


def across_rows(left, right):
    return lax.dot_general(
        left, right, (((0,), (0,)), ((), ())), preferred_element_type=jnp.float32
    )


def against_rows(left, right):
    return lax.dot_general(
        left, right, (((1,), (1,)), ((), ())), preferred_element_type=jnp.float32
    )


def windows():
    for start in range(0, SEQ_LEN, ROWS):
        yield start, max(0, start - LONGEST), start + ROWS


def turn(value, cosine, sine):
    return value * cosine + pltpu.roll(value, HD // 2, 1) * sine


def turn_back(value, cosine, sine):
    return value * cosine - pltpu.roll(value, HD // 2, 1) * sine


def fill_mask(mask_ref, segment_column, segment_row):
    for start, first, end in windows():
        rows = start + lax.broadcasted_iota(jnp.int32, (ROWS, end - first), 0)
        columns = first + lax.broadcasted_iota(jnp.int32, (ROWS, end - first), 1)
        same = segment_column[start:end, :] == segment_row[:, first:end]
        mask_ref[start:end, 0 : end - first] = jnp.where(
            same & (columns <= rows), 1.0, 0.0
        )


def attention_forward_kernel(
    acts, w_query, w_key, w_value, gain_query, gain_key, cosine, sine, seg_col, seg_row,
    query_normed, key_normed, values, attended, stats, mask,
):
    @pl.when(pl.program_id(0) == 0)
    def _():
        fill_mask(mask, seg_col, seg_row)

    cos, sin = cosine[...], sine[...]
    key = dot(acts[...], w_key[...])
    key_factor = lax.rsqrt(jnp.mean(key * key, axis=-1, keepdims=True) + norm_epsilon)
    key = key * key_factor
    key_normed[...] = key.astype(jnp.bfloat16)
    key = turn(key * gain_key[...], cos, sin).astype(jnp.bfloat16)
    value = dot(acts[...], w_value[...]).astype(jnp.bfloat16)
    values[...] = value
    stats[0, :, 4:5] = key_factor
    raw = dot(acts[...], w_query[...])
    for head in range(H // KV):
        lanes = slice(head * HD, (head + 1) * HD)
        query = raw[:, lanes]
        factor = lax.rsqrt(jnp.mean(query * query, axis=-1, keepdims=True) + norm_epsilon)
        query = query * factor
        query_normed[:, lanes] = query.astype(jnp.bfloat16)
        query = turn(query * gain_query[...], cos, sin).astype(jnp.bfloat16)
        stats[0, :, head : head + 1] = factor
        for start, first, end in windows():
            scores = against_rows(query[start:end], key[first:end])
            weights = jnp.exp(scores) * mask[start:end, 0 : end - first]
            total = jnp.sum(weights, axis=-1, keepdims=True)
            summed = dot(weights.astype(jnp.bfloat16), value[first:end])
            attended[start:end, lanes] = (summed / total).astype(jnp.bfloat16)
            stats[0, start:end, 2 + head : 3 + head] = jnp.log(total)


def attention_backward_kernel(
    acts_turned, grad_attn, w_query, w_key, w_value, w_output, gain_query, gain_key,
    cosine, sine, seg_col, seg_row, query_normed, key_normed, values, attended, stats, before,
    grad_wquery, grad_wkey, grad_wvalue, grad_acts, grad_gain_query, grad_gain_key,
    mask, grad_key, grad_value, grad_query, turned_back,
):
    scale = HD ** (-0.5)

    @pl.when(pl.program_id(0) == 0)
    def _():
        fill_mask(mask, seg_col, seg_row)
        grad_acts[...] = before[...]
        grad_gain_query[...] = jnp.zeros_like(grad_gain_query)
        grad_gain_key[...] = jnp.zeros_like(grad_gain_key)

    cos, sin = cosine[...], sine[...]
    grad_out = against_rows(grad_attn[...], w_output[...]).astype(jnp.bfloat16)
    normed = key_normed[...].astype(jnp.float32)
    key = turn(normed * gain_key[...], cos, sin).astype(jnp.bfloat16)
    value = values[...]
    grad_key[...] = jnp.zeros_like(grad_key)
    grad_value[...] = jnp.zeros_like(grad_value)
    for head in range(H // KV):
        lanes = slice(head * HD, (head + 1) * HD)
        normed = query_normed[:, lanes].astype(jnp.float32)
        query = turn(normed * (gain_query[...] * scale), cos, sin).astype(jnp.bfloat16)
        grad_head = grad_out[:, lanes]
        delta = jnp.sum(
            grad_head.astype(jnp.float32) * attended[:, lanes].astype(jnp.float32),
            axis=-1,
            keepdims=True,
        )
        for start, first, end in windows():
            scores = against_rows(query[start:end], key[first:end])
            probs = (
                jnp.exp(scores - stats[0, start:end, 2 + head : 3 + head])
                * mask[start:end, 0 : end - first]
            )
            grad_probs = against_rows(grad_head[start:end], value[first:end])
            grad_scores = (probs * (grad_probs - delta[start:end])).astype(jnp.bfloat16)
            turned_back[start:end, :] = dot(grad_scores, key[first:end]) * scale
            grad_key[first:end, :] += across_rows(grad_scores, query[start:end])
            grad_value[first:end, :] += across_rows(
                probs.astype(jnp.bfloat16), grad_head[start:end]
            )
        turned = turn_back(turned_back[...], cos, sin)
        grad_gain_query[...] += jnp.sum(turned * normed, axis=0, keepdims=True)
        turned = turned * gain_query[...]
        inner = jnp.mean(turned * normed, axis=-1, keepdims=True)
        grad_query[:, lanes] = (
            stats[0, :, head : head + 1] * (turned - normed * inner)
        ).astype(jnp.bfloat16)
    normed = key_normed[...].astype(jnp.float32)
    turned = turn_back(grad_key[...], cos, sin)
    grad_gain_key[...] += jnp.sum(turned * normed, axis=0, keepdims=True)
    turned = turned * gain_key[...]
    inner = jnp.mean(turned * normed, axis=-1, keepdims=True)
    low_key = (stats[0, :, 4:5] * (turned - normed * inner)).astype(jnp.bfloat16)
    low_value = grad_value[...].astype(jnp.bfloat16)
    low_query = grad_query[...]
    grad_wquery[...] = dot(acts_turned[...], low_query).astype(jnp.bfloat16)
    grad_wkey[...] = dot(acts_turned[...], low_key).astype(jnp.bfloat16)
    grad_wvalue[...] = dot(acts_turned[...], low_value).astype(jnp.bfloat16)
    grad_acts[...] += (
        against_rows(low_query, w_query[...])
        + against_rows(low_key, w_key[...])
        + against_rows(low_value, w_value[...])
    )


def feedforward_kernel(
    acts, acts_turned, branch, w_gate, w_up, w_down,
    summed, grad_acts, grad_wgate, grad_wup, grad_wdown,
):
    @pl.when(pl.program_id(0) == 0)
    def _():
        summed[...] = jnp.zeros_like(summed)
        grad_acts[...] = jnp.zeros_like(grad_acts)

    gate = dot(acts[...], w_gate[...])
    up = dot(acts[...], w_up[...])
    sigmoid = jax.nn.sigmoid(gate)
    swish = gate * sigmoid
    hidden = (swish * up).astype(jnp.bfloat16)
    summed[...] += dot(hidden, w_down[...])
    grad_hidden = against_rows(branch[...], w_down[...])
    grad_up = (grad_hidden * swish).astype(jnp.bfloat16)
    grad_gate = (grad_hidden * up * (sigmoid + swish * (1.0 - sigmoid))).astype(jnp.bfloat16)
    grad_wdown[...] = across_rows(hidden, branch[...]).astype(jnp.bfloat16)
    grad_wgate[...] = dot(acts_turned[...], grad_gate).astype(jnp.bfloat16)
    grad_wup[...] = dot(acts_turned[...], grad_up).astype(jnp.bfloat16)
    grad_acts[...] += against_rows(grad_gate, w_gate[...]) + against_rows(grad_up, w_up[...])


def whole(shape):
    return pl.BlockSpec(shape, lambda step: (0,) * len(shape))


def columns(rows, width, first=0):
    return pl.BlockSpec((rows, width), lambda step: (0, step + first))


def sds(shape, dtype=jnp.bfloat16):
    return jax.ShapeDtypeStruct(shape, dtype)


def params():
    return pltpu.CompilerParams(
        dimension_semantics=("arbitrary",), vmem_limit_bytes=VMEM_LIMIT
    )


def attention_forward(acts, w_query, w_key, w_value, tables):
    rows, width = acts.shape
    return pl.pallas_call(
        attention_forward_kernel,
        grid=(KV,),
        in_specs=[
            whole((rows, width)), columns(width, PAIR), columns(width, HD), columns(width, HD),
            whole((1, HD)), whole((1, HD)), whole((rows, HD)), whole((rows, HD)),
            whole((rows, 1)), whole((1, rows)),
        ],
        out_specs=[
            columns(rows, PAIR), columns(rows, HD), columns(rows, HD), columns(rows, PAIR),
            pl.BlockSpec((1, rows, 8), lambda step: (step, 0, 0)),
        ],
        out_shape=[
            sds((rows, H * HD)), sds((rows, KV * HD)), sds((rows, KV * HD)),
            sds((rows, H * HD)), sds((KV, rows, 8), jnp.float32),
        ],
        scratch_shapes=[pltpu.VMEM((rows, WINDOW), jnp.float32)],
        compiler_params=params(),
        cost_estimate=pl.CostEstimate(
            flops=2 * rows * width * 4096 + 6 * 10**9,
            bytes_accessed=26 * 2**20,
            transcendentals=10**7,
        ),
        name="attention_forward",
    )(acts, w_query, w_key, w_value, *tables)


def attention_backward(acts_turned, grad_attn, weights, tables, kept, before, first, count):
    w_query, w_key, w_value, w_output = weights
    rows, width = grad_attn.shape
    return pl.pallas_call(
        attention_backward_kernel,
        grid=(count,),
        in_specs=[
            whole((width, rows)), whole((rows, width)),
            columns(width, PAIR, first), columns(width, HD, first), columns(width, HD, first),
            pl.BlockSpec((PAIR, width), lambda step: (step + first, 0)),
            whole((1, HD)), whole((1, HD)), whole((rows, HD)), whole((rows, HD)),
            whole((rows, 1)), whole((1, rows)),
            columns(rows, PAIR, first), columns(rows, HD, first), columns(rows, HD, first),
            columns(rows, PAIR, first),
            pl.BlockSpec((1, rows, 8), lambda step: (step + first, 0, 0)),
            whole((rows, width)),
        ],
        out_specs=[
            columns(width, PAIR), columns(width, HD), columns(width, HD),
            whole((rows, width)), whole((1, HD)), whole((1, HD)),
        ],
        out_shape=[
            sds((width, count * PAIR)), sds((width, count * HD)), sds((width, count * HD)),
            sds((rows, width), jnp.float32), sds((1, HD), jnp.float32),
            sds((1, HD), jnp.float32),
        ],
        scratch_shapes=[
            pltpu.VMEM((rows, WINDOW), jnp.float32),
            pltpu.VMEM((rows, HD), jnp.float32),
            pltpu.VMEM((rows, HD), jnp.float32),
            pltpu.VMEM((rows, PAIR), jnp.bfloat16),
            pltpu.VMEM((rows, HD), jnp.float32),
        ],
        compiler_params=params(),
        cost_estimate=pl.CostEstimate(
            flops=(2 * rows * width * 1280 + 2 * 10**9) * count,
            bytes_accessed=(5 * count + 12) * 2**20,
            transcendentals=count * 10**6,
        ),
        name="attention_backward",
    )(acts_turned, grad_attn, w_query, w_key, w_value, w_output, *tables, *kept, before)


def feedforward(acts, acts_turned, branch, w_gate, w_up, w_down):
    rows, width = acts.shape
    units = w_gate.shape[1]
    down_spec = pl.BlockSpec((ROWS, width), lambda step: (step, 0))
    return pl.pallas_call(
        feedforward_kernel,
        grid=(units // ROWS,),
        in_specs=[
            whole((rows, width)), whole((width, rows)), whole((rows, width)),
            columns(width, ROWS), columns(width, ROWS), down_spec,
        ],
        out_specs=[
            whole((rows, width)), whole((rows, width)),
            columns(width, ROWS), columns(width, ROWS), down_spec,
        ],
        out_shape=[
            sds((rows, width), jnp.float32), sds((rows, width), jnp.float32),
            sds((width, units)), sds((width, units)), sds((units, width)),
        ],
        compiler_params=params(),
        cost_estimate=pl.CostEstimate(
            flops=18 * rows * width * units, bytes_accessed=52 * 2**20,
            transcendentals=rows * units,
        ),
        name="feedforward",
    )(acts, acts_turned, branch, w_gate, w_up, w_down)


def add_up(parts):
    total = parts[0].astype(jnp.float32)
    for part in parts[1:]:
        total = total + part.astype(jnp.float32)
    return total


def swap(value, axis, bit):
    size = lax.axis_size(axis)
    return lax.ppermute(value, axis, [(i, i ^ (1 << bit)) for i in range(size)])


def bits_of(axis):
    return lax.axis_size(axis).bit_length() - 1


def my_bit(axis, bit):
    return (lax.axis_index(axis) >> bit) & 1


def halve(value, axis, order):
    count = bits_of(axis)
    rows, width = value.shape
    value = value.reshape((2,) * count + (rows >> count, width))
    left = list(range(count))[::-1]
    for bit in order:
        place = left.index(bit)
        left.remove(bit)
        mine = my_bit(axis, bit)
        theirs = swap(lax.dynamic_index_in_dim(value, 1 - mine, place, False), axis, bit)
        own = lax.dynamic_index_in_dim(value, mine, place, False)
        value = (own.astype(jnp.float32) + theirs.astype(jnp.float32)).astype(value.dtype)
    return value


def double(value, axis, order):
    left = []
    for bit in order[::-1]:
        place = sum(1 for other in left if other > bit)
        left.append(bit)
        theirs = swap(value, axis, bit)
        mine = my_bit(axis, bit) == 0
        value = jnp.stack(
            [jnp.where(mine, value, theirs), jnp.where(mine, theirs, value)], place
        )
    return value.reshape((-1, value.shape[-1]))


def reduce_rows(parts, late):
    owned = halve(
        add_up(parts).astype(jnp.bfloat16), "shard", list(range(bits_of("shard")))
    )
    order = list(range(bits_of("replica")))
    order = order[1:] + order[:1] if late else order
    return double(halve(owned, "replica", order), "replica", order)


def sum_everywhere(value):
    for axis in ("shard", "replica"):
        for bit in range(bits_of(axis)):
            value = value + swap(value, axis, bit)
    return value


def shards(
    tokens, lengths, attention_gain, query_weight, key_weight, value_weight, query_gain,
    key_gain, output_weight, feedforward_gain, gate_weight, up_weight, down_weight, cotangent,
):
    def gather(array):
        return lax.all_gather(array, "shard", axis=0, tiled=True)

    gains = lax.all_gather(
        jnp.concatenate([attention_gain, feedforward_gain, query_gain, key_gain]), "shard", axis=0
    ).astype(jnp.float32)
    slim, narrow = attention_gain.shape[0], query_gain.shape[0]
    gain_one = gains[:, :slim].reshape(-1)
    gain_two = gains[:, slim : 2 * slim].reshape(-1)
    gain_query = gains[:, 2 * slim : 2 * slim + narrow].reshape(1, -1)
    gain_key = gains[:, 2 * slim + narrow :].reshape(1, -1)
    w_key, w_value, w_query = gather(key_weight), gather(value_weight), gather(query_weight)
    w_output = gather(output_weight)
    w_gate, w_up, w_down = gather(gate_weight), gather(up_weight), gather(down_weight)
    segment, position = doc_layout(lengths, SEQ_LEN)
    cosine, sine = rotary_tables(position, HD)
    half = HD // 2
    sine = jnp.concatenate([-sine[..., :half], sine[..., half:]], -1)
    scale = HD ** (-0.5)
    local_seqs = lengths.shape[0]
    x = tokens.astype(jnp.float32).reshape(local_seqs, SEQ_LEN, -1)
    dy = cotangent.reshape(local_seqs, SEQ_LEN, -1)
    seqs = range(local_seqs)
    mixed, states = [], []
    grads_gate, grads_up, grads_down, gain_two_terms = [], [], [], []
    for s in seqs:
        normed, factor_one = norm_forward(x[s], gain_one)
        acts = normed.astype(jnp.bfloat16)
        tables = (cosine[s], sine[s], segment[s][:, None], segment[s][None, :])
        query_normed, key_normed, values, attended, stats = attention_forward(
            acts, w_query, w_key, w_value, (gain_query * scale, gain_key, *tables)
        )
        middle = x[s] + dot(attended, w_output)
        normed_two, factor_two = norm_forward(middle, gain_two)
        acts_two = normed_two.astype(jnp.bfloat16)
        summed, grad_acts_two, grad_wgate, grad_wup, grad_wdown = feedforward(
            acts_two, acts_two.T, dy[s], w_gate, w_up, w_down
        )
        mixed.append((middle + summed).astype(jnp.bfloat16))
        grads_gate.append(grad_wgate)
        grads_up.append(grad_wup)
        grads_down.append(grad_wdown)
        grad_norm_two, terms = norm_backward(middle, factor_two, gain_two, grad_acts_two)
        gain_two_terms.append(jnp.sum(terms, axis=0))
        grad_middle = dy[s].astype(jnp.float32) + grad_norm_two
        kept = (query_normed, key_normed, values, attended, stats)
        states.append((acts, factor_one, tables, kept, grad_middle))
    out_gate, out_up = reduce_rows(grads_gate, False), reduce_rows(grads_up, True)
    out_down = reduce_rows(grads_down, True)
    low = [state[4].astype(jnp.bfloat16) for state in states]
    out_output = reduce_rows([across_rows(states[s][3][3], low[s]) for s in seqs], False)
    weights = (w_query, w_key, w_value, w_output)
    turned = [state[0].T for state in states]
    grad_acts = [jnp.zeros((SEQ_LEN, tokens.shape[1]), jnp.float32) for s in seqs]
    gain_query_terms, gain_key_terms = [], []
    outs = []
    count = KV // PARTS
    for part in range(PARTS):
        grads = []
        for s in seqs:
            tables = (gain_query, gain_key, *states[s][2])
            *weight_grads, grad_acts[s], query_term, key_term = attention_backward(
                turned[s], low[s], weights, tables, states[s][3], grad_acts[s], part * count, count
            )
            grads.append(weight_grads)
            gain_query_terms.append(query_term[0])
            gain_key_terms.append(key_term[0])
        outs.append([add_up(parts).astype(jnp.bfloat16) for parts in zip(*grads)])
    grads = [jnp.concatenate(parts, axis=1) for parts in zip(*outs)]
    out_query = reduce_rows(grads[:1], False).astype(jnp.float32)
    both = reduce_rows([jnp.concatenate(grads[1:], axis=1)], True).astype(jnp.float32)
    out_key, out_value = both[:, : KV * HD], both[:, KV * HD :]
    grad_tokens, gain_one_terms = [], []
    for s in seqs:
        grad_norm_one, terms = norm_backward(x[s], states[s][1], gain_one, grad_acts[s])
        gain_one_terms.append(jnp.sum(terms, axis=0))
        grad_tokens.append(states[s][4] + grad_norm_one)
    small = sum_everywhere(
        jnp.concatenate(
            [add_up(t) for t in (gain_one_terms, gain_two_terms, gain_query_terms, gain_key_terms)]
        ).reshape(-1, HD)
    ).reshape(-1)
    place = lax.axis_index("shard")
    model = slim * lax.axis_size("shard")

    def own(start, size):
        return lax.dynamic_slice(small, (start + place * size,), (size,))

    return (
        jnp.concatenate(mixed),
        jnp.concatenate(grad_tokens),
        own(0, slim),
        out_query,
        out_key,
        out_value,
        own(2 * model, narrow),
        own(2 * model + HD, narrow),
        out_output.astype(jnp.float32),
        own(model, slim),
        out_gate.astype(jnp.float32),
        out_up.astype(jnp.float32),
        out_down.astype(jnp.float32),
    )


def solution(mesh):
    return jax.shard_map(
        shards,
        mesh=mesh,
        in_specs=(
            P(("replica", "shard"), None),
            P(("replica", "shard"), None),
            P("shard"),
            P("shard", None),
            P("shard", None),
            P("shard", None),
            P("shard"),
            P("shard"),
            P("shard", None),
            P("shard"),
            P("shard", None),
            P("shard", None),
            P("shard", None),
            P(("replica", "shard"), None),
        ),
        out_specs=(
            P(("replica", "shard"), None),
            P(("replica", "shard"), None),
            P("shard"),
            P("shard", None),
            P("shard", None),
            P("shard", None),
            P("shard"),
            P("shard"),
            P("shard", None),
            P("shard"),
            P("shard", None),
            P("shard", None),
            P("shard", None),
        ),
        check_vma=False,
    )
```
